32 devices in a mesh: seq: 2 (over x), tensor: 16 (over z, y, core).
Axes of the slice: x: 2, y: 2, z: 4, core: 2. Of those that a mesh axis runs over, the one named last changes fastest.
Arguments:
- tokens: bfloat16 [768, 8192], P('tensor', 'seq'), may hold values from -6 to 6
- w_gate: bfloat16 [8192, 28672], P('seq', 'tensor'), may hold values from -0.109375 to 0.109375
- w_up: bfloat16 [8192, 28672], P('seq', 'tensor'), may hold values from -0.109375 to 0.109375
- w_down: bfloat16 [28672, 8192], P('tensor', 'seq'), may hold values from -0.0546875 to 0.0546875
- mask_gate: int32 [64, 224], P('seq', 'tensor'), may hold values 0 or 1
- mask_up: int32 [64, 224], P('seq', 'tensor'), may hold values 0 or 1
- mask_down: int32 [224, 64], P('tensor', 'seq'), may hold values 0 or 1
- cotangent: bfloat16 [768, 8192], P('tensor', 'seq'), may hold values from -6 to 6
Outputs:
- output: bfloat16 [768, 8192], P('tensor', 'seq')
- grad_tokens: bfloat16 [768, 8192], P('tensor', 'seq')
- grad_gate: bfloat16 [8192, 28672], P('seq', 'tensor')
- grad_up: bfloat16 [8192, 28672], P('seq', 'tensor')
- grad_down: bfloat16 [28672, 8192], P('tensor', 'seq')
The draws below stay inside these ranges and needn't reach their ends.
All inputs are finite; a program needn't handle non-finite values. No bound on the sum of `mask_gate` or of `mask_up` or of `mask_down` on one device may be relied on, other than what follows from the above.
Results may differ from the reference program's by a relative error of at most 0.0049.
Values may be sent and summed in bfloat16 or wider, within the bound.
No kernel may reach another device: no remote copies, remote signals or barrier semaphores. Data moves between devices by JAX's collectives and lax.ppermute only.
A program may use at most 320 MiB of HBM per device.

```python
import jax
import jax.numpy as jnp

D = 8192
FF = 28672
BLK = 128
TOKENS = 768


def set_ends(result, rng, least, high):
    dims = result.shape
    index_at = [jax.random.randint(jax.random.fold_in(rng, axis), (), 0, dims[axis]) for axis in range(len(dims))]
    result = result.at[tuple(index_at)].set(least)
    longest = dims.index(max(dims))
    index_at[longest] = (index_at[longest] + 1) % dims[longest]
    return result.at[tuple(index_at)].set(high)


def block_levels(own_key, shape, shards, low, largest):
    def one(dim, parts):
        heights = jax.random.uniform(jax.random.fold_in(jax.random.fold_in(own_key, 6), dim), (parts,), jnp.float32, low / len(shards), largest / len(shards))
        return jnp.repeat(jnp.exp(heights), shape[dim] // parts).reshape((-1,) + (1,) * (len(shape) - dim - 1))

    loudness = one(*shards[0])
    for cut in shards[1:]:
        loudness = loudness * one(*cut)
    return loudness


def bell_draw(own_key, dims, scale, most, cuts=(), held_as=jnp.bfloat16):
    gain = block_levels(own_key, dims, cuts, -0.22, 0.18) if cuts else 1.0
    array = jax.random.normal(own_key, dims, jnp.float32) * scale * gain
    return jnp.minimum(jnp.maximum(array, -most), most).astype(held_as)


def setup_inputs(seed: int = 0) -> dict:
    key_of = jax.random.split(jax.random.key(seed), 9)
    return {
        "tokens": bell_draw(key_of[0], (TOKENS, D), 1.0, 6.0, ((0, 16), (1, 2))),
        "w_gate": bell_draw(key_of[1], (D, FF), (2 * D // 5) ** -0.5, 0.109375, ((0, 2), (1, 16))),
        "w_up": bell_draw(key_of[2], (D, FF), (2 * D // 5) ** -0.5, 0.109375, ((0, 2), (1, 16))),
        "w_down": bell_draw(key_of[3], (FF, D), (2 * FF // 5) ** -0.5, 0.0546875, ((0, 16), (1, 2))),
        "mask_gate": set_ends((jax.random.randint(key_of[4], (D // BLK, FF // BLK), 0, 5) < 2).astype(jnp.int32), jax.random.fold_in(key_of[4], 1), 0, 1),
        "mask_up": set_ends((jax.random.randint(key_of[5], (D // BLK, FF // BLK), 0, 5) < 2).astype(jnp.int32), jax.random.fold_in(key_of[5], 1), 0, 1),
        "mask_down": set_ends((jax.random.randint(key_of[6], (FF // BLK, D // BLK), 0, 5) < 2).astype(jnp.int32), jax.random.fold_in(key_of[6], 1), 0, 1),
        "cotangent": bell_draw(key_of[7], (TOKENS, D), 1.0, 6.0, ((0, 16), (1, 2))),
    }


def widen(mask):
    full = jnp.repeat(jnp.repeat(mask, BLK, axis=0), BLK, axis=1)
    return full.astype(jnp.bfloat16)


def reference(tokens, w_gate, w_up, w_down, mask_gate, mask_up, mask_down, cotangent):
    gate_mask = widen(mask_gate)
    up_mask = widen(mask_up)
    down_mask = widen(mask_down)
    gate_w = w_gate * gate_mask
    up_w = w_up * up_mask
    down_w = w_down * down_mask
    gate = jnp.dot(tokens, gate_w, preferred_element_type=jnp.float32)
    up = jnp.dot(tokens, up_w, preferred_element_type=jnp.float32)
    sig = jax.nn.sigmoid(gate)
    act = gate * sig
    hidden = (act * up).astype(jnp.bfloat16)
    output = jnp.dot(hidden, down_w, preferred_element_type=jnp.float32).astype(jnp.bfloat16)
    grad_hidden = jnp.dot(cotangent, down_w.T, preferred_element_type=jnp.float32)
    dgate = (grad_hidden * up * sig * (1.0 + gate * (1.0 - sig))).astype(jnp.bfloat16)
    dup = (grad_hidden * act).astype(jnp.bfloat16)
    grad_tokens = (jnp.dot(dgate, gate_w.T, preferred_element_type=jnp.float32)
                   + jnp.dot(dup, up_w.T, preferred_element_type=jnp.float32)).astype(jnp.bfloat16)
    grad_gate = (jnp.dot(tokens.T, dgate, preferred_element_type=jnp.float32) * gate_mask).astype(jnp.bfloat16)
    grad_up = (jnp.dot(tokens.T, dup, preferred_element_type=jnp.float32) * up_mask).astype(jnp.bfloat16)
    grad_down = (jnp.dot(hidden.T, cotangent, preferred_element_type=jnp.float32) * down_mask).astype(jnp.bfloat16)
    return output, grad_tokens, grad_gate, grad_up, grad_down
```

```python
import jax
import jax.numpy as jnp
from jax import lax
from jax.experimental import pallas as pl
from jax.experimental.pallas import tpu as pltpu
from jax.sharding import PartitionSpec as P

BF = jnp.bfloat16
F32 = jnp.float32
BLK = 128
VMEM_LIMIT = 60 * 1024 * 1024


def cost(flops, read, written):
    return pl.CostEstimate(flops=flops // 1, bytes_accessed=(read + written) // 1, transcendentals=0)


def params():
    return pltpu.CompilerParams(
        dimension_semantics=("arbitrary",), vmem_limit_bytes=VMEM_LIMIT
    )


def pick(size, largest):
    best = BLK
    for blocks in range(1, largest // BLK + 1):
        if size % (blocks * BLK) == 0:
            best = blocks * BLK
    return best


def masked_tile(w_ref, mask_ref, row, rows, col, cols, mask_row, mask_col):
    strips = []
    for i in range(rows // BLK):
        parts = []
        for j in range(cols // BLK):
            keep = mask_ref[mask_row + i, mask_col + j].astype(F32)
            part = w_ref[row + i * BLK : row + (i + 1) * BLK, col + j * BLK : col + (j + 1) * BLK]
            parts.append(part * jnp.full((BLK, BLK), keep, F32).astype(BF))
        strips.append(parts[0] if len(parts) == 1 else jnp.concatenate(parts, axis=1))
    return strips[0] if len(strips) == 1 else jnp.concatenate(strips, axis=0)


def store(core_ref, rows, outs, total):
    if outs[0].shape[0] == total.shape[0]:
        for out in outs:
            out[...] = total.astype(out.dtype)
        return
    each = [total[at : at + rows] for at in range(0, total.shape[0], rows)]
    even, odd = jnp.concatenate(each[0::2], axis=0), jnp.concatenate(each[1::2], axis=0)
    first = core_ref[0] == 0
    outs[0][...] = jnp.where(first, even, odd).astype(outs[0].dtype)
    outs[1][...] = jnp.where(first, odd, even).astype(outs[1].dtype)


def whole_block(x):
    return pl.BlockSpec(x.shape, lambda j: (0, 0))


SMEM = pl.BlockSpec(memory_space=pltpu.SMEM)
UNREAD = pl.BlockSpec(memory_space=pl.ANY)


def take_kernel(x_ref, *refs):
    refs[-1][...] = x_ref[...]


def take(x, c, rows, after):
    return pl.pallas_call(
        take_kernel,
        grid=(1,),
        in_specs=[pl.BlockSpec((rows, x.shape[1]), lambda j: (c, 0))] + [UNREAD] * len(after),
        out_specs=pl.BlockSpec((rows, x.shape[1]), lambda j: (0, 0)),
        out_shape=jax.ShapeDtypeStruct((rows, x.shape[1]), x.dtype),
        compiler_params=params(),
        name="take_rows",
    )(x, *after)


def nn_kernel(rows, mask_ref, core_ref, x_ref, w_ref, *refs):
    outs = refs[-2:]
    depth, width = w_ref.shape
    step = pick(depth, 512)
    first = pl.program_id(0) * (width // BLK)
    total = None
    for k in range(0, depth, step):
        w = masked_tile(w_ref, mask_ref, k, step, 0, width, k // BLK, first)
        part = jnp.dot(x_ref[:, k : k + step], w, preferred_element_type=F32)
        total = part if total is None else total + part
    store(core_ref, rows, outs, total)


def nn(core, each, x, w, mask, takes, tile, after):
    rows, (depth, width) = x.shape[0], w.shape
    tile = pick(width, tile)
    return pl.pallas_call(
        lambda *refs: nn_kernel(each, *refs),
        grid=(width // tile,),
        in_specs=[SMEM, SMEM, whole_block(x), pl.BlockSpec((depth, tile), lambda j: (0, j))]
        + [UNREAD] * len(after),
        out_specs=[pl.BlockSpec((r, tile), lambda j: (0, j)) for r, _ in takes],
        out_shape=[jax.ShapeDtypeStruct((r, width), t) for r, t in takes],
        compiler_params=params(),
        cost_estimate=cost(2 * rows * depth * width, 2 * (depth * width + rows * depth), 4 * rows * width),
        name="times_masked",
    )(mask, core, x, w, *after)


def nt_kernel(rows, terms, core_ref, *refs):
    total = None
    for n in range(terms):
        mask_ref, x_ref, w_ref = refs[3 * n : 3 * n + 3]
        height, depth = w_ref.shape
        first = pl.program_id(0) * (height // BLK)
        step = pick(depth, 512)
        for k in range(0, depth, step):
            w = masked_tile(w_ref, mask_ref, 0, height, k, step, first, k // BLK)
            part = lax.dot_general(
                x_ref[:, k : k + step], w, (((1,), (1,)), ((), ())), preferred_element_type=F32
            )
            total = part if total is None else total + part
    store(core_ref, rows, refs[-2:], total)


def nt(core, each, terms, takes, tile, after):
    rows = terms[0][0].shape[0]
    height, depth = terms[0][1].shape
    tile = pick(height, tile)
    specs, args = [SMEM], [core]
    for x, w, mask in terms:
        specs += [SMEM, whole_block(x), pl.BlockSpec((tile, depth), lambda j: (j, 0))]
        args += [mask, x, w]
    n = len(terms)
    return pl.pallas_call(
        lambda *refs: nt_kernel(each, n, *refs),
        grid=(height // tile,),
        in_specs=specs + [UNREAD] * len(after),
        out_specs=[pl.BlockSpec((r, tile), lambda j: (0, j)) for r, _ in takes],
        out_shape=[jax.ShapeDtypeStruct((r, height), t) for r, t in takes],
        compiler_params=params(),
        cost_estimate=cost(
            2 * n * rows * depth * height, 2 * n * (depth * height + rows * depth), 4 * rows * height
        ),
        name="times_masked_transposed",
    )(*args, *after)


def tn_kernel(chunks, mask_ref, *refs):
    xs, ds = refs[:chunks], refs[chunks : 2 * chunks]
    out, turned = refs[-chunks - 1], refs[-chunks:]
    height, width = out.shape
    first = pl.program_id(0) * (height // BLK)
    for x, t in zip(xs, turned):
        t[...] = x[...].T
    step = pick(width, 256)
    for n in range(0, width, step):
        total = None
        for t, d in zip(turned, ds):
            part = jnp.dot(t[...], d[:, n : n + step], preferred_element_type=F32)
            total = part if total is None else total + part
        for i in range(height // BLK):
            for j in range(step // BLK):
                keep = mask_ref[first + i, n // BLK + j].astype(F32)
                out[i * BLK : (i + 1) * BLK, n + j * BLK : n + (j + 1) * BLK] = (
                    total[i * BLK : (i + 1) * BLK, j * BLK : (j + 1) * BLK] * keep
                ).astype(BF)


def tn(xs, ds, mask, tile, after):
    chunks = len(xs)
    (rows, height), width = xs[0].shape, ds[0].shape[1]
    tile = pick(height, tile)
    return pl.pallas_call(
        lambda *refs: tn_kernel(chunks, *refs),
        grid=(height // tile,),
        in_specs=[SMEM]
        + [pl.BlockSpec((rows, tile), lambda i: (0, i)) for _ in xs]
        + [whole_block(d) for d in ds]
        + [UNREAD] * len(after),
        out_specs=pl.BlockSpec((tile, width), lambda i: (i, 0)),
        out_shape=jax.ShapeDtypeStruct((height, width), BF),
        scratch_shapes=[pltpu.VMEM((tile, rows), BF) for _ in xs],
        compiler_params=params(),
        cost_estimate=cost(
            2 * chunks * rows * height * width, 2 * chunks * rows * (height + width), 2 * height * width
        ),
        name="weight_grad",
    )(mask, *xs, *ds, *after)


def added(refs):
    total = refs[0][...]
    for ref in refs[1:]:
        total = total + ref[...].astype(F32)
    return total


def hidden_kernel(n, *refs):
    gate, up = added(refs[:n]), added(refs[n : 2 * n])
    refs[-1][...] = (gate * jax.nn.sigmoid(gate) * up).astype(BF)


def grads_kernel(n, *refs):
    gate, up, dh = added(refs[:n]), added(refs[n : 2 * n]), added(refs[2 * n : 3 * n])
    sig = jax.nn.sigmoid(gate)
    refs[-2][...] = (dh * up * sig * (1.0 + gate * (1.0 - sig))).astype(BF)
    refs[-1][...] = (dh * (gate * sig)).astype(BF)


def gating(kernel, sums, outs, after):
    rows, width = sums[0][0].shape
    tile = pick(width, 256)
    spec = pl.BlockSpec((rows, tile), lambda j: (0, j))
    flat = [part for parts in sums for part in parts]
    return pl.pallas_call(
        lambda *refs: kernel(len(sums[0]), *refs),
        grid=(width // tile,),
        in_specs=[spec] * len(flat) + [UNREAD] * len(after),
        out_specs=[spec] * outs,
        out_shape=[jax.ShapeDtypeStruct((rows, width), BF)] * outs,
        compiler_params=params(),
        cost_estimate=cost(20 * rows * width, 6 * len(sums) * rows * width, 2 * outs * rows * width),
        name="gating",
    )(*flat, *after)


def solution(mesh):
    size = mesh.shape["seq"]
    spread = mesh.shape["tensor"]
    chunks = 3

    def per_device(tokens, w_gate, w_up, w_down, mask_gate, mask_up, mask_down, cotangent):
        rows = tokens.shape[0] // chunks
        total = rows * spread
        cores = [(i, i ^ 1) for i in range(spread)]
        same_core = [list(range(core, spread, 2)) for core in range(2)]
        whole = ((total, F32), (total, BF))
        split = ((total // 2, F32), (total // 2, BF))
        core = jnp.reshape(lax.axis_index("tensor") % 2, (1,)).astype(jnp.int32)
        last = [mask_gate]

        def run(kernel, *args, late=()):
            out = kernel(*args, [last[0], *late])
            last[0] = out[0] if isinstance(out, (tuple, list)) else out
            return out

        def gather(x, c):
            return lax.all_gather(run(take, x, c, rows), "tensor", axis=0, tiled=True)

        def scatter(mine, others):
            both = mine + lax.ppermute(others, "tensor", cores).astype(F32)
            return lax.psum_scatter(
                both, "tensor", scatter_dimension=0, tiled=True, axis_index_groups=same_core
            ).astype(BF)

        arrived = []

        def exchange(own, sent):
            shifts = [[(i, (i + k) % size) for i in range(size)] for k in range(1, size)]
            parts = [lax.ppermute(sent, "seq", shift) for shift in shifts]
            arrived.append(parts)
            return [own] + parts

        def late():
            return arrived[-2] if len(arrived) > 1 else []

        toks, cots, gates, ups, dhs, hiddens, dgates, dups, outs, gtoks = ([] for _ in range(10))

        def gate_sums(c):
            gates.append(
                exchange(*run(nn, core, rows, toks[c], w_gate, mask_gate, whole, 256, late=late()))
            )

        def up_sums(c):
            ups.append(exchange(*run(nn, core, rows, toks[c], w_up, mask_up, whole, 256, late=late())))

        def dh_sums(c):
            terms = [(cots[c], w_down, mask_down)]
            dhs.append(exchange(*run(nt, core, rows, terms, whole, 256, late=late())))

        def back_out(c):
            (hidden,) = run(gating, hidden_kernel, [gates[c], ups[c]], 1)
            hiddens.append(hidden)
            outs.append(scatter(*run(nn, core, rows, hidden, w_down, mask_down, split, 512)))

        def back_tokens(c):
            dgate, dup = run(gating, grads_kernel, [gates[c], ups[c], dhs[c]], 2)
            dgates.append(dgate)
            dups.append(dup)
            terms = [(dgate, w_gate, mask_gate), (dup, w_up, mask_up)]
            gtoks.append(scatter(*run(nt, core, rows, terms, split, 512)))

        toks.append(gather(tokens, 0))
        cots.append(gather(cotangent, 0))
        gate_sums(0)
        toks.append(gather(tokens, 1))
        up_sums(0)
        cots.append(gather(cotangent, 1))
        dh_sums(0)
        toks.append(gather(tokens, 2))
        gate_sums(1)
        cots.append(gather(cotangent, 2))
        back_out(0)
        up_sums(1)
        back_tokens(0)
        dh_sums(1)
        gate_sums(2)
        back_out(1)
        up_sums(2)
        back_tokens(1)
        dh_sums(2)
        back_out(2)
        grad_down = run(tn, hiddens, cots, mask_down, 256)
        back_tokens(2)
        grad_gate = run(tn, toks, dgates, mask_gate, 512)
        grad_up = run(tn, toks, dups, mask_up, 512)
        output = jnp.concatenate(outs, axis=0)
        grad_tokens = jnp.concatenate(gtoks, axis=0)
        return (output, grad_tokens, grad_gate, grad_up, grad_down)

    return jax.shard_map(
        per_device,
        mesh=mesh,
        in_specs=(
            P("tensor", "seq"),
            P("seq", "tensor"),
            P("seq", "tensor"),
            P("tensor", "seq"),
            P("seq", "tensor"),
            P("seq", "tensor"),
            P("tensor", "seq"),
            P("tensor", "seq"),
        ),
        out_specs=(
            P("tensor", "seq"),
            P("tensor", "seq"),
            P("seq", "tensor"),
            P("seq", "tensor"),
            P("tensor", "seq"),
        ),
        check_vma=False,
    )
```

```python
import jax
import jax.numpy as jnp
from jax import lax
from jax.experimental import pallas as pl
from jax.experimental.pallas import tpu as pltpu
from jax.sharding import PartitionSpec as P

BF = jnp.bfloat16
F32 = jnp.float32
BLK = 128
SHARE = 2
VMEM_LIMIT = 60 * 1024 * 1024


def cost(flops, read, written):
    return pl.CostEstimate(flops=flops // SHARE, bytes_accessed=(read + written) // SHARE, transcendentals=0)


def params():
    return pltpu.CompilerParams(
        dimension_semantics=("arbitrary",), vmem_limit_bytes=VMEM_LIMIT
    )


def pick(size, largest):
    best = BLK
    for blocks in range(1, largest // BLK + 1):
        if size % (blocks * BLK) == 0:
            best = blocks * BLK
    return best


def mask_kernel(mask_ref, w_ref, *refs):
    for j in range(w_ref.shape[1] // BLK):
        keep = mask_ref[pl.program_id(0), j].astype(F32)
        block = slice(j * BLK, (j + 1) * BLK)
        refs[-1][:, block] = (w_ref[:, block].astype(F32) * keep).astype(BF)


def masked(w, mask, after):
    block = pl.BlockSpec((BLK, w.shape[1]), lambda i: (i, 0))
    return pl.pallas_call(
        mask_kernel,
        grid=(w.shape[0] // BLK,),
        in_specs=[SMEM, block] + [UNREAD] * len(after),
        out_specs=block,
        out_shape=jax.ShapeDtypeStruct(w.shape, BF),
        compiler_params=params(),
        cost_estimate=cost(w.size, 2 * w.size, 2 * w.size),
        name="masked_weights",
    )(mask, w, *after)


def reversed_bits(value, count):
    result = 0
    for _ in range(count):
        result = result * 2 + value % 2
        value = value // 2
    return result


def store(place_ref, outs, ordered, total):
    if not ordered:
        for out in outs:
            out[...] = total.astype(out.dtype)
        return
    turned = ordered[0]
    devices, rows = turned.shape[:2]
    bits = devices.bit_length() - 1
    for r in range(devices):
        turned[lax.bitwise_xor(place_ref[0], reversed_bits(r, bits))] = total[r * rows : (r + 1) * rows]
    outs[0][...] = turned[: devices // 2]
    outs[1][...] = turned[devices // 2 :].astype(BF)


def whole_block(x):
    return pl.BlockSpec(x.shape, lambda j: (0, 0))


SMEM = pl.BlockSpec(memory_space=pltpu.SMEM)
UNREAD = pl.BlockSpec(memory_space=pl.ANY)


def product_kernel(terms, contract, by_device, place_ref, *refs):
    total = None
    for n in range(terms):
        part = lax.dot_general(
            refs[2 * n][...], refs[2 * n + 1][...], (((1,), (contract,)), ((), ())), preferred_element_type=F32
        )
        total = part if total is None else total + part
    at = len(refs) - by_device
    store(place_ref, refs[at - 2 : at], refs[at:], total)


def product(contract, place, devices, terms, tile, after):
    rows = terms[0][0].shape[0]
    width = terms[0][1].shape[1 - contract]
    depth = terms[0][1].shape[contract]
    tile = pick(width, tile)
    specs, args = [SMEM], [place]
    for x, w in terms:
        if contract:
            specs += [whole_block(x), pl.BlockSpec((tile, depth), lambda j: (j, 0))]
        else:
            specs += [whole_block(x), pl.BlockSpec((depth, tile), lambda j: (0, j))]
        args += [x, w]
    scratch = []
    if devices:
        each = rows // devices
        shape = (devices // 2, each, width)
        out_spec = pl.BlockSpec((devices // 2, each, tile), lambda j: (0, 0, j))
        scratch = [pltpu.VMEM((devices, each, tile), F32)]
    else:
        shape, out_spec = (rows, width), pl.BlockSpec((rows, tile), lambda j: (0, j))
    n = len(terms)
    return pl.pallas_call(
        lambda *refs: product_kernel(n, contract, len(scratch), *refs),
        grid=(width // tile,),
        in_specs=specs + [UNREAD] * len(after),
        out_specs=[out_spec, out_spec],
        out_shape=[jax.ShapeDtypeStruct(shape, F32), jax.ShapeDtypeStruct(shape, BF)],
        scratch_shapes=scratch,
        compiler_params=params(),
        cost_estimate=cost(
            2 * n * rows * depth * width, 2 * n * (depth * width + rows * depth), 4 * rows * width
        ),
        name="product",
    )(*args, *after)


def tn_kernel(chunks, mask_ref, *refs):
    xs, ds = refs[:chunks], refs[chunks : 2 * chunks]
    out, turned = refs[-chunks - 1], refs[-chunks:]
    height, width = out.shape
    first = pl.program_id(0) * (height // BLK)
    for x, t in zip(xs, turned):
        t[...] = x[...].T
    step = pick(width, 256)
    for n in range(0, width, step):
        total = None
        for t, d in zip(turned, ds):
            part = jnp.dot(t[...], d[:, n : n + step], preferred_element_type=F32)
            total = part if total is None else total + part
        for i in range(height // BLK):
            for j in range(step // BLK):
                keep = mask_ref[first + i, n // BLK + j].astype(F32)
                out[i * BLK : (i + 1) * BLK, n + j * BLK : n + (j + 1) * BLK] = (
                    total[i * BLK : (i + 1) * BLK, j * BLK : (j + 1) * BLK] * keep
                ).astype(BF)


def tn(xs, ds, mask, tile, after):
    chunks = len(xs)
    height, width = xs[0].shape[1], ds[0].shape[1]
    rows = sum(x.shape[0] for x in xs)
    tile = pick(height, tile)
    return pl.pallas_call(
        lambda *refs: tn_kernel(chunks, *refs),
        grid=(height // tile,),
        in_specs=[SMEM]
        + [pl.BlockSpec((x.shape[0], tile), lambda i: (0, i)) for x in xs]
        + [whole_block(d) for d in ds]
        + [UNREAD] * len(after),
        out_specs=pl.BlockSpec((tile, width), lambda i: (i, 0)),
        out_shape=jax.ShapeDtypeStruct((height, width), BF),
        scratch_shapes=[pltpu.VMEM((tile, x.shape[0]), BF) for x in xs],
        compiler_params=params(),
        cost_estimate=cost(
            2 * rows * height * width, 2 * rows * (height + width), 2 * height * width
        ),
        name="weight_grad",
    )(mask, *xs, *ds, *after)


def added(refs):
    total = refs[0][...]
    for ref in refs[1:]:
        total = total + ref[...].astype(F32)
    return total


def hidden_kernel(n, *refs):
    gate, up = added(refs[:n]), added(refs[n : 2 * n])
    refs[-1][...] = (gate * jax.nn.sigmoid(gate) * up).astype(BF)


def grads_kernel(n, *refs):
    gate, up, dh = added(refs[:n]), added(refs[n : 2 * n]), added(refs[2 * n : 3 * n])
    sig = jax.nn.sigmoid(gate)
    refs[-2][...] = (dh * up * sig * (1.0 + gate * (1.0 - sig))).astype(BF)
    refs[-1][...] = (dh * (gate * sig)).astype(BF)


def gating(kernel, sums, outs, after):
    rows, width = sums[0][0].shape
    tile = pick(width, 256)
    spec = pl.BlockSpec((rows, tile), lambda j: (0, j))
    flat = [part for parts in sums for part in parts]
    return pl.pallas_call(
        lambda *refs: kernel(len(sums[0]), *refs),
        grid=(width // tile,),
        in_specs=[spec] * len(flat) + [UNREAD] * len(after),
        out_specs=[spec] * outs,
        out_shape=[jax.ShapeDtypeStruct((rows, width), BF)] * outs,
        compiler_params=params(),
        cost_estimate=cost(20 * rows * width, 6 * len(sums) * rows * width, 2 * outs * rows * width),
        name="gating",
    )(*flat, *after)


def stage_kernel(mine_ref, got_ref, *refs):
    both = mine_ref[...] + got_ref[...].astype(F32)
    half = both.shape[0] // 2
    if half:
        refs[-2][...] = both[:half]
        refs[-1][...] = both[half:].astype(BF)
    else:
        refs[-1][...] = both.astype(BF)


def stage(mine, got, after):
    count, rows, width = mine.shape
    tile = pick(width, 1024)
    made = [(count // 2, F32), (count // 2, BF)] if count > 1 else [(count, BF)]
    block = lambda n: pl.BlockSpec((n, rows, tile), lambda j: (0, 0, j))
    return pl.pallas_call(
        stage_kernel,
        grid=(width // tile,),
        in_specs=[block(count), block(count)] + [UNREAD] * len(after),
        out_specs=[block(n) for n, _ in made],
        out_shape=[jax.ShapeDtypeStruct((n, rows, width), t) for n, t in made],
        compiler_params=params(),
        cost_estimate=cost(mine.size, 6 * mine.size, 3 * mine.size),
        name="stage",
    )(mine, got, *after)


def solution(mesh):
    size = mesh.shape["seq"]
    spread = mesh.shape["tensor"]
    bits = spread.bit_length() - 1
    FIRST, SECOND = 0, 1

    def per_device(tokens, w_gate, w_up, w_down, mask_gate, mask_up, mask_down, cotangent):
        third = tokens.shape[0] // 3
        parts = [(0, 2 * third), (2 * third, 3 * third)]
        index = lax.axis_index("tensor")
        place = jnp.reshape(reversed_bits(index, bits), (1,)).astype(jnp.int32)
        last = [mask_gate]

        def run(kernel, *args, late=()):
            out = kernel(*args, [last[0], *late])
            last[0] = out[0] if isinstance(out, (tuple, list)) else out
            return out

        def gather(x, c):
            return lax.all_gather(x[parts[c][0] : parts[c][1]], "tensor", axis=0, tiled=True)

        moving, done = [], {}

        def halving(name, mine, others):
            for bit in range(bits):
                pairs = [(i, i ^ (1 << bit)) for i in range(spread)]
                got = lax.ppermute(others, "tensor", pairs)
                yield
                sums = run(stage, mine, got)
                if len(sums) == 2:
                    mine, others = sums
            done[name] = sums[0][0]

        def start(name, sums):
            moving.append(halving(name, *sums))
            next(moving[-1])

        def advance():
            for sums in list(moving):
                next(sums, None)

        arrived = []

        def exchange(own, sent):
            shifts = [[(i, (i + k) % size) for i in range(size)] for k in range(1, size)]
            got = [lax.ppermute(sent, "seq", shift) for shift in shifts]
            arrived.append(got)
            return [own] + got

        def late():
            return arrived[-2] if len(arrived) > 1 else []

        toks = [gather(tokens, c) for c in range(2)]
        cots = [gather(cotangent, c) for c in range(2)]
        gate_w = run(masked, w_gate, mask_gate)
        up_w = run(masked, w_up, mask_up)
        down_w = run(masked, w_down, mask_down)
        hiddens, dgates, dups = [], [], []

        def ahead(x, w, contract):
            return exchange(*run(product, contract, place, 0, [(x, w)], 256, late=late()))

        def back_out(name, gate, up, wait):
            (hidden,) = run(gating, hidden_kernel, [gate, up], 1)
            hiddens.append(hidden)
            terms = [(hidden, down_w)]
            sums = run(product, 0, place, spread, terms, 512, late=wait)
            advance()
            start(name, sums)

        def back_tokens(name, gate, up, dh):
            dgate, dup = run(gating, grads_kernel, [gate, up, dh], 2)
            dgates.append(dgate)
            dups.append(dup)
            terms = [(dgate, gate_w), (dup, up_w)]
            sums = run(product, 1, place, spread, terms, 512)
            advance()
            start(name, sums)

        gates, ups, dhs = [], [], []
        for c in (FIRST, SECOND):
            gates.append(ahead(toks[c], gate_w, 0))
            ups.append(ahead(toks[c], up_w, 0))
        dhs.append(ahead(cots[FIRST], down_w, 1))
        back_out("out", gates[FIRST], ups[FIRST], [cots[SECOND], *arrived[3]])
        dhs.append(ahead(cots[SECOND], down_w, 1))
        advance()
        back_out("out last", gates[SECOND], ups[SECOND], arrived[4])
        back_tokens("tokens", gates[FIRST], ups[FIRST], dhs[FIRST])
        back_tokens("tokens last", gates[SECOND], ups[SECOND], dhs[SECOND])
        grad_down = run(tn, hiddens, cots, mask_down, 256)
        advance()
        grad_gate = run(tn, toks, dgates, mask_gate, 512)
        advance()
        grad_up = run(tn, toks, dups, mask_up, 512)
        while len(done) < 4:
            advance()
        output = jnp.concatenate([done["out"], done["out last"]], axis=0)
        grad_tokens = jnp.concatenate([done["tokens"], done["tokens last"]], axis=0)
        return (output, grad_tokens, grad_gate, grad_up, grad_down)

    return jax.shard_map(
        per_device,
        mesh=mesh,
        in_specs=(
            P("tensor", "seq"),
            P("seq", "tensor"),
            P("seq", "tensor"),
            P("tensor", "seq"),
            P("seq", "tensor"),
            P("seq", "tensor"),
            P("tensor", "seq"),
            P("tensor", "seq"),
        ),
        out_specs=(
            P("tensor", "seq"),
            P("tensor", "seq"),
            P("seq", "tensor"),
            P("seq", "tensor"),
            P("tensor", "seq"),
        ),
        check_vma=False,
    )
```

```python
import jax
import jax.numpy as jnp
from jax import lax
from jax.experimental import pallas as pl
from jax.experimental.pallas import tpu as pltpu
from jax.sharding import PartitionSpec as P

BF = jnp.bfloat16
F32 = jnp.float32
BLK = 128
SHARE = 2
VMEM_LIMIT = 60 * 1024 * 1024


def cost(flops, read, written):
    return pl.CostEstimate(flops=flops // SHARE, bytes_accessed=(read + written) // SHARE, transcendentals=0)


def params():
    return pltpu.CompilerParams(
        dimension_semantics=("arbitrary",), vmem_limit_bytes=VMEM_LIMIT
    )


def pick(size, largest):
    best = BLK
    for blocks in range(1, largest // BLK + 1):
        if size % (blocks * BLK) == 0:
            best = blocks * BLK
    return best


def mask_kernel(mask_ref, w_ref, *refs):
    blocks = w_ref.shape[0] // BLK
    for i in range(blocks):
        for j in range(w_ref.shape[1] // BLK):
            keep = mask_ref[pl.program_id(0) * blocks + i, j].astype(F32)
            block = (slice(i * BLK, (i + 1) * BLK), slice(j * BLK, (j + 1) * BLK))
            refs[-1][block] = (w_ref[block].astype(F32) * keep).astype(BF)


def masked(w, mask, after):
    tall = pick(w.shape[0], 2 * 1024 * 1024 // w.shape[1])
    block = pl.BlockSpec((tall, w.shape[1]), lambda i: (i, 0))
    return pl.pallas_call(
        mask_kernel,
        grid=(w.shape[0] // tall,),
        in_specs=[SMEM, block] + [UNREAD] * len(after),
        out_specs=block,
        out_shape=jax.ShapeDtypeStruct(w.shape, BF),
        compiler_params=params(),
        cost_estimate=cost(w.size, 2 * w.size, 2 * w.size),
        name="masked_weights",
    )(mask, w, *after)


def reversed_bits(value, count):
    result = 0
    for _ in range(count):
        result = result * 2 + value % 2
        value = value // 2
    return result


def store(place_ref, outs, ordered, total):
    if not ordered:
        for out in outs:
            out[...] = total.astype(out.dtype)
        return
    turned = ordered[0]
    devices, rows = turned.shape[:2]
    bits = devices.bit_length() - 1
    for r in range(devices):
        turned[lax.bitwise_xor(place_ref[0], reversed_bits(r, bits))] = total[r * rows : (r + 1) * rows]
    outs[0][...] = turned[: devices // 2]
    outs[1][...] = turned[devices // 2 :].astype(BF)


def whole_block(x):
    return pl.BlockSpec(x.shape, lambda j: (0, 0))


SMEM = pl.BlockSpec(memory_space=pltpu.SMEM)
UNREAD = pl.BlockSpec(memory_space=pl.ANY)


def product_kernel(terms, contract, by_device, place_ref, *refs):
    total = None
    for n in range(terms):
        part = lax.dot_general(
            refs[2 * n][...], refs[2 * n + 1][...], (((1,), (contract,)), ((), ())), preferred_element_type=F32
        )
        total = part if total is None else total + part
    at = len(refs) - by_device
    store(place_ref, refs[at - 2 : at], refs[at:], total)


def product(contract, place, devices, terms, tile, after):
    rows = terms[0][0].shape[0]
    width = terms[0][1].shape[1 - contract]
    depth = terms[0][1].shape[contract]
    tile = pick(width, tile)
    specs, args = [SMEM], [place]
    for x, w in terms:
        if contract:
            specs += [whole_block(x), pl.BlockSpec((tile, depth), lambda j: (j, 0))]
        else:
            specs += [whole_block(x), pl.BlockSpec((depth, tile), lambda j: (0, j))]
        args += [x, w]
    scratch = []
    if devices:
        each = rows // devices
        shape = (devices // 2, each, width)
        out_spec = pl.BlockSpec((devices // 2, each, tile), lambda j: (0, 0, j))
        scratch = [pltpu.VMEM((devices, each, tile), F32)]
    else:
        shape, out_spec = (rows, width), pl.BlockSpec((rows, tile), lambda j: (0, j))
    n = len(terms)
    return pl.pallas_call(
        lambda *refs: product_kernel(n, contract, len(scratch), *refs),
        grid=(width // tile,),
        in_specs=specs + [UNREAD] * len(after),
        out_specs=[out_spec, out_spec],
        out_shape=[jax.ShapeDtypeStruct(shape, F32), jax.ShapeDtypeStruct(shape, BF)],
        scratch_shapes=scratch,
        compiler_params=params(),
        cost_estimate=cost(
            2 * n * rows * depth * width, 2 * n * (depth * width + rows * depth), 4 * rows * width
        ),
        name="product",
    )(*args, *after)


def tn_kernel(chunks, mask_ref, *refs):
    xs, ds = refs[:chunks], refs[chunks : 2 * chunks]
    out, turned = refs[-chunks - 1], refs[-chunks:]
    height, width = out.shape
    first = pl.program_id(0) * (height // BLK)
    for x, t in zip(xs, turned):
        t[...] = x[...].T
    step = pick(width, 256)
    for n in range(0, width, step):
        total = None
        for t, d in zip(turned, ds):
            part = jnp.dot(t[...], d[:, n : n + step], preferred_element_type=F32)
            total = part if total is None else total + part
        for i in range(height // BLK):
            for j in range(step // BLK):
                keep = mask_ref[first + i, n // BLK + j].astype(F32)
                out[i * BLK : (i + 1) * BLK, n + j * BLK : n + (j + 1) * BLK] = (
                    total[i * BLK : (i + 1) * BLK, j * BLK : (j + 1) * BLK] * keep
                ).astype(BF)


def tn(xs, ds, mask, tile, after):
    chunks = len(xs)
    height, width = xs[0].shape[1], ds[0].shape[1]
    rows = sum(x.shape[0] for x in xs)
    tile = pick(height, tile)
    return pl.pallas_call(
        lambda *refs: tn_kernel(chunks, *refs),
        grid=(height // tile,),
        in_specs=[SMEM]
        + [pl.BlockSpec((x.shape[0], tile), lambda i: (0, i)) for x in xs]
        + [whole_block(d) for d in ds]
        + [UNREAD] * len(after),
        out_specs=pl.BlockSpec((tile, width), lambda i: (i, 0)),
        out_shape=jax.ShapeDtypeStruct((height, width), BF),
        scratch_shapes=[pltpu.VMEM((tile, x.shape[0]), BF) for x in xs],
        compiler_params=params(),
        cost_estimate=cost(
            2 * rows * height * width, 2 * rows * (height + width), 2 * height * width
        ),
        name="weight_grad",
    )(mask, *xs, *ds, *after)


def added(refs):
    total = refs[0][...]
    for ref in refs[1:]:
        total = total + ref[...].astype(F32)
    return total


def hidden_kernel(n, *refs):
    gate, up = added(refs[:n]), added(refs[n : 2 * n])
    refs[-1][...] = (gate * jax.nn.sigmoid(gate) * up).astype(BF)


def grads_kernel(n, *refs):
    gate, up, dh = added(refs[:n]), added(refs[n : 2 * n]), added(refs[2 * n : 3 * n])
    sig = jax.nn.sigmoid(gate)
    refs[-2][...] = (dh * up * sig * (1.0 + gate * (1.0 - sig))).astype(BF)
    refs[-1][...] = (dh * (gate * sig)).astype(BF)


def gating(kernel, sums, outs, after):
    rows, width = sums[0][0].shape
    tile = pick(width, 256)
    spec = pl.BlockSpec((rows, tile), lambda j: (0, j))
    flat = [part for parts in sums for part in parts]
    return pl.pallas_call(
        lambda *refs: kernel(len(sums[0]), *refs),
        grid=(width // tile,),
        in_specs=[spec] * len(flat) + [UNREAD] * len(after),
        out_specs=[spec] * outs,
        out_shape=[jax.ShapeDtypeStruct((rows, width), BF)] * outs,
        compiler_params=params(),
        cost_estimate=cost(20 * rows * width, 6 * len(sums) * rows * width, 2 * outs * rows * width),
        name="gating",
    )(*flat, *after)


def stage_kernel(mine_ref, got_ref, *refs):
    both = mine_ref[...] + got_ref[...].astype(F32)
    half = both.shape[0] // 2
    if half:
        refs[-2][...] = both[:half]
        refs[-1][...] = both[half:].astype(BF)
    else:
        refs[-1][...] = both.astype(BF)


def stage(mine, got, after):
    count, rows, width = mine.shape
    tile = pick(width, 256 * 1024 // (count * rows))
    made = [(count // 2, F32), (count // 2, BF)] if count > 1 else [(count, BF)]
    block = lambda n: pl.BlockSpec((n, rows, tile), lambda j: (0, 0, j))
    return pl.pallas_call(
        stage_kernel,
        grid=(width // tile,),
        in_specs=[block(count), block(count)] + [UNREAD] * len(after),
        out_specs=[block(n) for n, _ in made],
        out_shape=[jax.ShapeDtypeStruct((n, rows, width), t) for n, t in made],
        compiler_params=params(),
        cost_estimate=cost(mine.size, 6 * mine.size, 3 * mine.size),
        name="stage",
    )(mine, got, *after)


def solution(mesh):
    size = mesh.shape["seq"]
    spread = mesh.shape["tensor"]
    bits = spread.bit_length() - 1
    FIRST, SECOND = 0, 1

    def per_device(tokens, w_gate, w_up, w_down, mask_gate, mask_up, mask_down, cotangent):
        third = tokens.shape[0] // 3
        parts = [(0, 2 * third), (2 * third, 3 * third)]
        index = lax.axis_index("tensor")
        place = jnp.reshape(reversed_bits(index, bits), (1,)).astype(jnp.int32)
        last = [mask_gate]

        def run(kernel, *args, late=()):
            out = kernel(*args, [last[0], *late])
            last[0] = out[0] if isinstance(out, (tuple, list)) else out
            return out

        def gather(x, c):
            return lax.all_gather(x[parts[c][0] : parts[c][1]], "tensor", axis=0, tiled=True)

        moving, done = [], {}

        def halving(name, mine, others):
            for bit in range(bits):
                pairs = [(i, i ^ (1 << bit)) for i in range(spread)]
                got = lax.ppermute(others, "tensor", pairs)
                yield
                sums = run(stage, mine, got)
                if len(sums) == 2:
                    mine, others = sums
            done[name] = sums[0][0]

        def start(name, sums):
            moving.append(halving(name, *sums))
            next(moving[-1])

        def advance():
            for sums in list(moving):
                next(sums, None)

        arrived = []

        def exchange(own, sent):
            shifts = [[(i, (i + k) % size) for i in range(size)] for k in range(1, size)]
            got = [lax.ppermute(sent, "seq", shift) for shift in shifts]
            arrived.append(got)
            return [own] + got

        def late():
            return arrived[-2] if len(arrived) > 1 else []

        toks, cots = [], []
        for c in range(2):
            toks.append(gather(tokens, c))
            cots.append(gather(cotangent, c))
        gate_w = run(masked, w_gate, mask_gate)
        up_w = run(masked, w_up, mask_up)
        hiddens, dgates, dups = [], [], []

        def ahead(x, w, contract):
            return exchange(*run(product, contract, place, 0, [(x, w)], 256, late=late()))

        def back_out(name, wait):
            sums = run(product, 0, place, spread, [(hiddens[-1], down_w)], 512, late=wait)
            advance()
            start(name, sums)

        def back_tokens(name, dgate, dup):
            dgates.append(dgate)
            dups.append(dup)
            terms = [(dgate, gate_w), (dup, up_w)]
            sums = run(product, 1, place, spread, terms, 512)
            advance()
            start(name, sums)

        def make_hidden(c, wait):
            hiddens.extend(run(gating, hidden_kernel, [gates[c], ups[c]], 1, late=wait))

        def exchange_halves(own, sent):
            half = sent.shape[0] // 2
            first, last = exchange(own, sent[:half])[1:], exchange(own, sent[half:])[1:]
            return [own] + [jnp.concatenate(both, axis=0) for both in zip(first, last)], first

        gates, ups, dhs = [], [], []
        gates.append(ahead(toks[FIRST], gate_w, 0))
        ups.append(ahead(toks[FIRST], up_w, 0))
        down_w = run(masked, w_down, mask_down)
        sums = run(product, 1, place, 0, [(cots[FIRST], down_w)], 256, late=late())
        dh, first_half = exchange_halves(*sums)
        dhs.append(dh)
        gates.append(exchange(*run(product, 0, place, 0, [(toks[SECOND], gate_w)], 256, late=arrived[1])))
        make_hidden(FIRST, [])
        back_out("out", [cots[SECOND], *first_half])
        ups.append(exchange(*run(product, 0, place, 0, [(toks[SECOND], up_w)], 256)))
        advance()
        dgrads = run(gating, grads_kernel, [gates[FIRST], ups[FIRST], dhs[FIRST]], 2)
        sums = run(product, 1, place, 0, [(cots[SECOND], down_w)], 256, late=gates[SECOND][1:])
        dhs.append(exchange(*sums))
        advance()
        back_tokens("tokens", *dgrads)
        make_hidden(SECOND, [])
        back_out("out last", [])
        dgrads = run(gating, grads_kernel, [gates[SECOND], ups[SECOND], dhs[SECOND]], 2)
        back_tokens("tokens last", *dgrads)
        grad_down = run(tn, hiddens, cots, mask_down, 256)
        advance()
        grad_gate = run(tn, toks, dgates, mask_gate, 512)
        advance()
        grad_up = run(tn, toks, dups, mask_up, 512)
        while len(done) < 4:
            advance()
        output = jnp.concatenate([done["out"], done["out last"]], axis=0)
        grad_tokens = jnp.concatenate([done["tokens"], done["tokens last"]], axis=0)
        return (output, grad_tokens, grad_gate, grad_up, grad_down)

    return jax.shard_map(
        per_device,
        mesh=mesh,
        in_specs=(
            P("tensor", "seq"),
            P("seq", "tensor"),
            P("seq", "tensor"),
            P("tensor", "seq"),
            P("seq", "tensor"),
            P("seq", "tensor"),
            P("tensor", "seq"),
            P("tensor", "seq"),
        ),
        out_specs=(
            P("tensor", "seq"),
            P("tensor", "seq"),
            P("seq", "tensor"),
            P("seq", "tensor"),
            P("tensor", "seq"),
        ),
        check_vma=False,
    )
```

```python
import jax
import jax.numpy as jnp
from jax import lax
from jax.experimental import pallas as pl
from jax.experimental.pallas import tpu as pltpu
from jax.sharding import PartitionSpec as P

BF = jnp.bfloat16
F32 = jnp.float32
BLK = 128
SHARE = 2
VMEM_LIMIT = 60 * 1024 * 1024


def cost(flops, read, written):
    return pl.CostEstimate(flops=flops // SHARE, bytes_accessed=(read + written) // SHARE, transcendentals=0)


def params():
    return pltpu.CompilerParams(
        dimension_semantics=("arbitrary",), vmem_limit_bytes=VMEM_LIMIT
    )


def pick(size, largest):
    best = BLK
    for blocks in range(1, largest // BLK + 1):
        if size % (blocks * BLK) == 0:
            best = blocks * BLK
    return best


def mask_kernel(mask_ref, w_ref, *refs):
    blocks = w_ref.shape[0] // BLK
    for i in range(blocks):
        for j in range(w_ref.shape[1] // BLK):
            keep = mask_ref[pl.program_id(0) * blocks + i, j].astype(F32)
            block = (slice(i * BLK, (i + 1) * BLK), slice(j * BLK, (j + 1) * BLK))
            refs[-1][block] = (w_ref[block].astype(F32) * keep).astype(BF)


def masked(w, mask, after):
    tall = pick(w.shape[0], 2 * 1024 * 1024 // w.shape[1])
    block = pl.BlockSpec((tall, w.shape[1]), lambda i: (i, 0))
    return pl.pallas_call(
        mask_kernel,
        grid=(w.shape[0] // tall,),
        in_specs=[SMEM, block] + [UNREAD] * len(after),
        out_specs=block,
        out_shape=jax.ShapeDtypeStruct(w.shape, BF),
        compiler_params=params(),
        cost_estimate=cost(w.size, 2 * w.size, 2 * w.size),
        name="masked_weights",
    )(mask, w, *after)


def reversed_bits(value, count):
    result = 0
    for _ in range(count):
        result = result * 2 + value % 2
        value = value // 2
    return result


def store(place_ref, outs, ordered, total):
    if not ordered:
        for out in outs:
            out[...] = total.astype(out.dtype)
        return
    turned = ordered[0]
    devices, rows = turned.shape[:2]
    bits = devices.bit_length() - 1
    for r in range(devices):
        turned[lax.bitwise_xor(place_ref[0], reversed_bits(r, bits))] = total[r * rows : (r + 1) * rows]
    outs[0][...] = turned[: devices // 2]
    outs[1][...] = turned[devices // 2 :].astype(BF)


def whole_block(x):
    return pl.BlockSpec(x.shape, lambda j: (0, 0))


SMEM = pl.BlockSpec(memory_space=pltpu.SMEM)
UNREAD = pl.BlockSpec(memory_space=pl.ANY)


def product_kernel(terms, contract, by_device, place_ref, *refs):
    total = None
    for n in range(terms):
        part = lax.dot_general(
            refs[2 * n][...], refs[2 * n + 1][...], (((1,), (contract,)), ((), ())), preferred_element_type=F32
        )
        total = part if total is None else total + part
    at = len(refs) - by_device
    store(place_ref, refs[at - 2 : at], refs[at:], total)


def product(contract, place, devices, terms, tile, after):
    rows = terms[0][0].shape[0]
    width = terms[0][1].shape[1 - contract]
    depth = terms[0][1].shape[contract]
    tile = pick(width, tile)
    specs, args = [SMEM], [place]
    for x, w in terms:
        if contract:
            specs += [whole_block(x), pl.BlockSpec((tile, depth), lambda j: (j, 0))]
        else:
            specs += [whole_block(x), pl.BlockSpec((depth, tile), lambda j: (0, j))]
        args += [x, w]
    scratch = []
    if devices:
        each = rows // devices
        shape = (devices // 2, each, width)
        out_spec = pl.BlockSpec((devices // 2, each, tile), lambda j: (0, 0, j))
        scratch = [pltpu.VMEM((devices, each, tile), F32)]
    else:
        shape, out_spec = (rows, width), pl.BlockSpec((rows, tile), lambda j: (0, j))
    n = len(terms)
    return pl.pallas_call(
        lambda *refs: product_kernel(n, contract, len(scratch), *refs),
        grid=(width // tile,),
        in_specs=specs + [UNREAD] * len(after),
        out_specs=[out_spec, out_spec],
        out_shape=[jax.ShapeDtypeStruct(shape, F32), jax.ShapeDtypeStruct(shape, BF)],
        scratch_shapes=scratch,
        compiler_params=params(),
        cost_estimate=cost(
            2 * n * rows * depth * width, 2 * n * (depth * width + rows * depth), 4 * rows * width
        ),
        name="product",
    )(*args, *after)


def tn_kernel(chunks, mask_ref, *refs):
    xs, ds = refs[:chunks], refs[chunks : 2 * chunks]
    out, turned = refs[-chunks - 1], refs[-chunks:]
    height, width = out.shape
    first = pl.program_id(0) * (height // BLK)
    for x, t in zip(xs, turned):
        t[...] = x[...].T
    step = pick(width, 256)
    for n in range(0, width, step):
        total = None
        for t, d in zip(turned, ds):
            part = jnp.dot(t[...], d[:, n : n + step], preferred_element_type=F32)
            total = part if total is None else total + part
        for i in range(height // BLK):
            for j in range(step // BLK):
                keep = mask_ref[first + i, n // BLK + j].astype(F32)
                out[i * BLK : (i + 1) * BLK, n + j * BLK : n + (j + 1) * BLK] = (
                    total[i * BLK : (i + 1) * BLK, j * BLK : (j + 1) * BLK] * keep
                ).astype(BF)


def tn(xs, ds, mask, tile, after):
    chunks = len(xs)
    height, width = xs[0].shape[1], ds[0].shape[1]
    rows = sum(x.shape[0] for x in xs)
    tile = pick(height, tile)
    return pl.pallas_call(
        lambda *refs: tn_kernel(chunks, *refs),
        grid=(height // tile,),
        in_specs=[SMEM]
        + [pl.BlockSpec((x.shape[0], tile), lambda i: (0, i)) for x in xs]
        + [whole_block(d) for d in ds]
        + [UNREAD] * len(after),
        out_specs=pl.BlockSpec((tile, width), lambda i: (i, 0)),
        out_shape=jax.ShapeDtypeStruct((height, width), BF),
        scratch_shapes=[pltpu.VMEM((tile, x.shape[0]), BF) for x in xs],
        compiler_params=params(),
        cost_estimate=cost(
            2 * rows * height * width, 2 * rows * (height + width), 2 * height * width
        ),
        name="weight_grad",
    )(mask, *xs, *ds, *after)


def added(refs):
    total = refs[0][...]
    for ref in refs[1:]:
        total = total + ref[...].astype(F32)
    return total


def hidden_kernel(n, *refs):
    gate, up = added(refs[:n]), added(refs[n : 2 * n])
    refs[-1][...] = (gate * jax.nn.sigmoid(gate) * up).astype(BF)


def grads_kernel(n, *refs):
    gate, up, dh = added(refs[:n]), added(refs[n : 2 * n]), added(refs[2 * n : 3 * n])
    sig = jax.nn.sigmoid(gate)
    refs[-2][...] = (dh * up * sig * (1.0 + gate * (1.0 - sig))).astype(BF)
    refs[-1][...] = (dh * (gate * sig)).astype(BF)


def gating(kernel, sums, outs, after):
    rows, width = sums[0][0].shape
    tile = pick(width, 256)
    spec = pl.BlockSpec((rows, tile), lambda j: (0, j))
    flat = [part for parts in sums for part in parts]
    return pl.pallas_call(
        lambda *refs: kernel(len(sums[0]), *refs),
        grid=(width // tile,),
        in_specs=[spec] * len(flat) + [UNREAD] * len(after),
        out_specs=[spec] * outs,
        out_shape=[jax.ShapeDtypeStruct((rows, width), BF)] * outs,
        compiler_params=params(),
        cost_estimate=cost(20 * rows * width, 6 * len(sums) * rows * width, 2 * outs * rows * width),
        name="gating",
    )(*flat, *after)


def stage_kernel(mine_ref, got_ref, *refs):
    both = mine_ref[...] + got_ref[...].astype(F32)
    half = both.shape[0] // 2
    if half:
        refs[-2][...] = both[:half]
        refs[-1][...] = both[half:].astype(BF)
    else:
        refs[-1][...] = both.astype(BF)


def stage(mine, got, after):
    count, rows, width = mine.shape
    tile = pick(width, 256 * 1024 // (count * rows))
    made = [(count // 2, F32), (count // 2, BF)] if count > 1 else [(count, BF)]
    block = lambda n: pl.BlockSpec((n, rows, tile), lambda j: (0, 0, j))
    return pl.pallas_call(
        stage_kernel,
        grid=(width // tile,),
        in_specs=[block(count), block(count)] + [UNREAD] * len(after),
        out_specs=[block(n) for n, _ in made],
        out_shape=[jax.ShapeDtypeStruct((n, rows, width), t) for n, t in made],
        compiler_params=params(),
        cost_estimate=cost(mine.size, 6 * mine.size, 3 * mine.size),
        name="stage",
    )(mine, got, *after)


def solution(mesh):
    size = mesh.shape["seq"]
    spread = mesh.shape["tensor"]
    bits = spread.bit_length() - 1
    FIRST, SECOND = 0, 1

    def per_device(tokens, w_gate, w_up, w_down, mask_gate, mask_up, mask_down, cotangent):
        third = tokens.shape[0] // 3
        parts = [(0, 2 * third), (2 * third, 3 * third)]
        index = lax.axis_index("tensor")
        place = jnp.reshape(reversed_bits(index, bits), (1,)).astype(jnp.int32)
        last = [mask_gate]

        def run(kernel, *args, late=()):
            out = kernel(*args, [last[0], *late])
            last[0] = out[0] if isinstance(out, (tuple, list)) else out
            return out

        def gather(x, c):
            return lax.all_gather(x[parts[c][0] : parts[c][1]], "tensor", axis=0, tiled=True)

        moving, done = [], {}

        def halving(name, mine, others):
            for bit in range(bits):
                pairs = [(i, i ^ (1 << bit)) for i in range(spread)]
                got = lax.ppermute(others, "tensor", pairs)
                yield
                sums = run(stage, mine, got)
                if len(sums) == 2:
                    mine, others = sums
            done[name] = sums[0][0]

        def start(name, sums):
            moving.append(halving(name, *sums))
            next(moving[-1])

        def advance():
            for sums in list(moving):
                next(sums, None)

        arrived = []

        def exchange(own, sent):
            shifts = [[(i, (i + k) % size) for i in range(size)] for k in range(1, size)]
            got = [lax.ppermute(sent, "seq", shift) for shift in shifts]
            arrived.append(got)
            return [own] + got

        def late():
            return arrived[-2] if len(arrived) > 1 else []

        toks, cots = [], []
        for c in range(2):
            toks.append(gather(tokens, c))
            cots.append(gather(cotangent, c))
        gate_w = run(masked, w_gate, mask_gate)
        up_w = run(masked, w_up, mask_up)
        hiddens, dgates, dups = [], [], []

        def ahead(x, w, contract):
            return exchange(*run(product, contract, place, 0, [(x, w)], 256, late=late()))

        def back_out(name, wait):
            sums = run(product, 0, place, spread, [(hiddens[-1], down_w)], 512, late=wait)
            advance()
            start(name, sums)

        def back_tokens(name, dgate, dup, onward):
            dgates.append(dgate)
            dups.append(dup)
            terms = [(dgate, gate_w), (dup, up_w)]
            sums = run(product, 1, place, spread, terms, 512)
            if onward:
                advance()
            start(name, sums)

        def make_hidden(c, wait):
            hiddens.extend(run(gating, hidden_kernel, [gates[c], ups[c]], 1, late=wait))

        def exchange_halves(own, sent):
            half = sent.shape[0] // 2
            first, last = exchange(own, sent[:half])[1:], exchange(own, sent[half:])[1:]
            return [own] + [jnp.concatenate(both, axis=0) for both in zip(first, last)], first

        gates, ups, dhs = [], [], []
        gates.append(ahead(toks[FIRST], gate_w, 0))
        ups.append(ahead(toks[FIRST], up_w, 0))
        down_w = run(masked, w_down, mask_down)
        sums = run(product, 1, place, 0, [(cots[FIRST], down_w)], 256, late=late())
        dh, first_half = exchange_halves(*sums)
        dhs.append(dh)
        gates.append(exchange(*run(product, 0, place, 0, [(toks[SECOND], gate_w)], 256, late=arrived[1])))
        make_hidden(FIRST, [])
        back_out("out", first_half)
        ups.append(exchange(*run(product, 0, place, 0, [(toks[SECOND], up_w)], 256, late=[cots[SECOND]])))
        advance()
        dgrads = run(gating, grads_kernel, [gates[FIRST], ups[FIRST], dhs[FIRST]], 2)
        sums = run(product, 1, place, 0, [(cots[SECOND], down_w)], 256, late=gates[SECOND][1:])
        dhs.append(exchange(*sums))
        advance()
        back_tokens("tokens", *dgrads, False)
        make_hidden(SECOND, [])
        back_out("out last", [])
        dgrads = run(gating, grads_kernel, [gates[SECOND], ups[SECOND], dhs[SECOND]], 2)
        back_tokens("tokens last", *dgrads, True)
        grad_down = run(tn, hiddens, cots, mask_down, 256)
        advance()
        grad_gate = run(tn, toks, dgates, mask_gate, 512)
        advance()
        grad_up = run(tn, toks, dups, mask_up, 512)
        while len(done) < 4:
            advance()
        output = jnp.concatenate([done["out"], done["out last"]], axis=0)
        grad_tokens = jnp.concatenate([done["tokens"], done["tokens last"]], axis=0)
        return (output, grad_tokens, grad_gate, grad_up, grad_down)

    return jax.shard_map(
        per_device,
        mesh=mesh,
        in_specs=(
            P("tensor", "seq"),
            P("seq", "tensor"),
            P("seq", "tensor"),
            P("tensor", "seq"),
            P("seq", "tensor"),
            P("seq", "tensor"),
            P("tensor", "seq"),
            P("tensor", "seq"),
        ),
        out_specs=(
            P("tensor", "seq"),
            P("tensor", "seq"),
            P("seq", "tensor"),
            P("seq", "tensor"),
            P("tensor", "seq"),
        ),
        check_vma=False,
    )
```
